32 devices in a mesh: group: 4 (over x, core), dp: 2 (over y), tensor: 4 (over z).
Axes of the slice: x: 2, y: 2, z: 4, core: 2. Of those that a mesh axis runs over, the one named last changes fastest.
Arguments:
- weight: float32 [14848, 8192], P('group', ('dp', 'tensor')), may hold values from -0.046875 to 0.046875
- moment: float32 [14848, 8192], P('group', ('dp', 'tensor')), may hold values from -1.8 to 1.8
- second: float32 [14848, 8192], P('group', ('dp', 'tensor')), may hold values from 0.02 to 0.3
- gradient: bfloat16 [14848, 8192], P('group', ('dp', 'tensor')), may hold values from -600 to 600
- hidden: bfloat16 [1024, 14848], P(('group', 'dp'), 'tensor'), may hold values from -6 to 6
- stream: bfloat16 [1024, 8192], P(('group', 'dp'), 'tensor'), may hold values from -32 to 32
- norm_gain: bfloat16 [8192], P('tensor'), may hold values from 0.25 to 1.75
Outputs:
- weight_new: float32 [14848, 8192], P('group', ('dp', 'tensor'))
- moment_new: float32 [14848, 8192], P('group', ('dp', 'tensor'))
- second_new: float32 [14848, 8192], P('group', ('dp', 'tensor'))
- normed: bfloat16 [1024, 8192], P(('group', 'dp'), 'tensor')
- residual: bfloat16 [1024, 8192], P(('group', 'dp'), 'tensor')
The draws below stay inside these ranges and needn't reach their ends.
All inputs are finite; a program needn't handle non-finite values.
Results may differ from the reference program's by a relative error of at most 0.0095.
Values may be sent and summed in bfloat16 or wider, within the bound.
A program may use at most 256 MiB of HBM per device.

```python
import math
import jax
import jax.numpy as jnp
from jax import lax

D = 8192
FFW = 14848
ROWS = 128
TOTAL_ROWS = 1024
N_GROUP = 4
N_DP = 2
N_TENSOR = 4


def draw_gradient(key, part):
    row_pos = jnp.arange(FFW, dtype=jnp.float32)[:, None] / FFW
    col_pos = jnp.arange(D, dtype=jnp.float32)[None, :] / D
    rising = jnp.exp(0.5 * jnp.log(3.0) * (row_pos + col_pos))
    values = jax.random.truncated_normal(key, -4.0, 4.0, (FFW, D), jnp.float32) * rising
    return values.astype(jnp.bfloat16)


def draw_stream(key, part):
    total_rows = ROWS * N_GROUP * N_DP
    col_pos = jnp.arange(D, dtype=jnp.float32)[None, :] / D
    key_base = jax.random.fold_in(jax.random.fold_in(key, 7), 0)
    rising = jnp.exp(jnp.log(3.0) * col_pos)
    values = jax.random.truncated_normal(key_base, -4.0, 4.0, (total_rows, D), jnp.float32) * rising
    return values.astype(jnp.bfloat16)


def block_scale(key, shape, cuts, least, high):
    gain, own = 1.0, jax.random.fold_in(key, 6)
    for dim, blocks in cuts:
        draws = jnp.exp(jax.random.uniform(jax.random.fold_in(own, dim), (blocks,), jnp.float32, least / len(cuts), high / len(cuts)))
        gain = gain * jnp.repeat(draws, shape[dim] // blocks).reshape([-1 if axis == dim else 1 for axis in range(len(shape))])
    return gain


def gaussian(rng, dims, deviation, limit, pieces=(), kind=jnp.bfloat16):
    drawn = jax.random.normal(rng, dims, jnp.float32) * deviation
    if len(pieces) > 0:
        drawn = block_scale(rng, dims, pieces, -0.22, 0.18) * drawn
    return jnp.clip(drawn, min=-limit, max=limit).astype(kind)


def setup_inputs(seed: int = 0) -> dict:
    seeds = jax.random.split(jax.random.key(seed), 8)
    return {
        "weight": gaussian(seeds[0], (FFW, D), FFW ** -0.5, 0.046875, ((0, 4), (1, 8)), jnp.float32),
        "moment": gaussian(seeds[1], (FFW, D), 0.3, 1.8, ((0, 4), (1, 8)), jnp.float32),
        "second": jnp.clip(jnp.exp(math.log(0.3) - 2.7080503 * jax.random.uniform(seeds[2], (FFW, D), jnp.float32) ** block_scale(seeds[2], (FFW, D), ((0, 4), (1, 8)), -0.2, 0.2)), 0.02, 0.3),
        "gradient": draw_gradient(jax.random.fold_in(seeds[7], 71), 0),
        "hidden": gaussian(seeds[4], (TOTAL_ROWS, FFW), 1.0, 6.0, ((0, 8), (1, 4))),
        "stream": draw_stream(jax.random.fold_in(seeds[7], 71), 0),
        "norm_gain": jnp.clip(1.0 + 0.15 * jax.random.normal(seeds[6], (D,), jnp.float32), 0.25, 1.75).astype(jnp.bfloat16),
    }


clip_rms = 0.5
beta_one = 0.9
beta_two = 0.95
bias_one = 1.0 - 0.9 ** 10
bias_two = 1.0 - 0.95 ** 10
adam_eps = 1e-08
learn_rate = 0.002

def reference(weight, moment, second, gradient, hidden, stream, norm_gain):
    grad_float = gradient.astype(jnp.float32)
    grad_total = jnp.sum(grad_float * grad_float)
    factor = jnp.minimum(1.0, clip_rms * jnp.sqrt(jnp.float32(FFW * D)) / (jnp.sqrt(grad_total) + 1e-06))
    clipped = factor * grad_float
    moment_new = beta_one * moment + (1.0 - beta_one) * clipped
    second_new = beta_two * second + (1.0 - beta_two) * clipped * clipped
    update = moment_new / bias_one / (jnp.sqrt(second_new / bias_two) + adam_eps)
    weight_new = weight - learn_rate * update
    shipped = weight_new.astype(jnp.bfloat16)
    slice_rows = FFW // N_TENSOR

    def accumulate(running, block_index):
        hidden_part = lax.dynamic_slice_in_dim(hidden, block_index * slice_rows, slice_rows, 1)
        weight_part = lax.dynamic_slice_in_dim(shipped, block_index * slice_rows, slice_rows, 0)
        product = jnp.dot(hidden_part, weight_part, preferred_element_type=jnp.float32)
        rounded = lax.optimization_barrier(product.astype(jnp.bfloat16))
        return (running + rounded.astype(jnp.float32), None)
    empty_sum = jnp.zeros((hidden.shape[0], D), jnp.float32)
    summed, _ = lax.scan(accumulate, empty_sum, jnp.arange(N_TENSOR, dtype=jnp.int32))
    residual_sum = stream.astype(jnp.float32) + summed
    squares = lax.optimization_barrier(jnp.sum(residual_sum * residual_sum, axis=1, keepdims=True))
    normed = residual_sum * lax.rsqrt(squares / D + 1e-06) * norm_gain.astype(jnp.float32)
    return (weight_new, moment_new, second_new, normed.astype(jnp.bfloat16), residual_sum.astype(jnp.bfloat16))
```

```python
import math

import jax
import jax.numpy as jnp
from jax import lax
from jax.sharding import PartitionSpec as P

AXES = ("group", "dp", "tensor")

clip_rms = 0.5
beta_one = 0.9
beta_two = 0.95
bias_one = 1.0 - 0.9**10
bias_two = 1.0 - 0.95**10
adam_eps = 1e-08
learn_rate = 0.002


def permute(value, sizes, target):
    groups, ranks, slices = sizes
    index = lambda g, d, t: (g * ranks + d) * slices + t
    pairs = [
        (index(g, d, t), index(*target(g, d, t)))
        for g in range(groups)
        for d in range(ranks)
        for t in range(slices)
    ]
    return lax.ppermute(value, AXES, pairs)


def gather_hidden(hidden, sizes):
    groups, ranks, slices = sizes
    rows, units = hidden.shape
    split = slices // groups
    moved = permute(
        hidden, sizes, lambda g, d, t: (t // split, d, g * split + t % split)
    )
    full = lax.all_gather(moved, ("dp", "tensor"), axis=0, tiled=True)
    if split == 1:
        return full
    full = full.reshape(ranks * groups, split, rows, units).transpose(0, 2, 1, 3)
    return full.reshape(ranks * groups * rows, split * units)


def per_device(weight, moment, second, gradient, hidden, stream, norm_gain):
    sizes = tuple(lax.axis_size(axis) for axis in AXES)
    groups, ranks, slices = sizes
    g, d, t = (lax.axis_index(axis) for axis in AXES)
    entries = weight.size * groups * ranks * slices
    width = stream.shape[1] * slices
    rows = stream.shape[0]

    activations = gather_hidden(hidden, sizes)

    grad_float = gradient.astype(jnp.float32)
    grad_total = lax.psum(jnp.sum(grad_float * grad_float), AXES)
    factor = jnp.minimum(1.0, clip_rms * math.sqrt(entries) / (jnp.sqrt(grad_total) + 1e-06))
    clipped = factor * grad_float
    moment_new = beta_one * moment + (1.0 - beta_one) * clipped
    second_new = beta_two * second + (1.0 - beta_two) * clipped * clipped
    update = moment_new / bias_one / (jnp.sqrt(second_new / bias_two) + adam_eps)
    weight_new = weight - learn_rate * update
    shipped = weight_new.astype(jnp.bfloat16)

    term = jnp.dot(activations, shipped, preferred_element_type=jnp.float32)
    cols = term.shape[1]
    part = term.astype(jnp.bfloat16).reshape(ranks, groups, rows, cols)

    step = groups // 2
    while step >= 1:
        bit = (g // step) % 2
        pairs = part.reshape(ranks, 2, -1, rows, cols)
        kept = lax.dynamic_index_in_dim(pairs, bit, 1, keepdims=False)
        sent = lax.dynamic_index_in_dim(pairs, 1 - bit, 1, keepdims=False)
        got = permute(sent, sizes, lambda g, d, t, step=step: (g ^ step, d, t))
        part = (kept.astype(jnp.float32) + got.astype(jnp.float32)).astype(jnp.bfloat16)
        step //= 2
    part = part.reshape(ranks, rows, cols)

    place = (d * slices + t) % ranks
    summed = jnp.zeros((ranks, rows, cols), jnp.bfloat16)
    for turn in range(ranks):
        sent = lax.dynamic_index_in_dim(part, (place + turn) % ranks, 0, keepdims=False)

        def target(g, d, t, turn=turn):
            block = d * slices + t
            return (g, (block % ranks + turn) % ranks, block // ranks)

        got = permute(sent, sizes, target)
        summed = lax.dynamic_update_index_in_dim(summed, got, (d - turn) % ranks, 0)
    summed = summed.transpose(1, 0, 2).reshape(rows, ranks * cols)

    residual_sum = stream.astype(jnp.float32) + summed.astype(jnp.float32)
    squares = lax.psum(jnp.sum(residual_sum * residual_sum, axis=1), "tensor")
    normed = residual_sum * lax.rsqrt(squares / width + 1e-06)[:, None] * norm_gain.astype(jnp.float32)
    return (
        weight_new,
        moment_new,
        second_new,
        normed.astype(jnp.bfloat16),
        residual_sum.astype(jnp.bfloat16),
    )


def solution(mesh):
    master = P("group", ("dp", "tensor"))
    decode = P(("group", "dp"), "tensor")
    return jax.shard_map(
        per_device,
        mesh=mesh,
        in_specs=(master, master, master, master, decode, decode, P("tensor")),
        out_specs=(master, master, master, decode, decode),
        check_vma=False,
    )
```

```python
import math

import jax
import jax.numpy as jnp
from jax import lax
from jax.sharding import PartitionSpec as P

AXES = ("group", "dp", "tensor")

clip_rms = 0.5
beta_one = 0.9
beta_two = 0.95
bias_one = 1.0 - 0.9**10
bias_two = 1.0 - 0.95**10
adam_eps = 1e-08
learn_rate = 0.002


def permute(value, sizes, target):
    groups, ranks, slices = sizes
    index = lambda g, d, t: (g * ranks + d) * slices + t
    pairs = [
        (index(g, d, t), index(*target(g, d, t)))
        for g in range(groups)
        for d in range(ranks)
        for t in range(slices)
    ]
    return lax.ppermute(value, AXES, pairs)


def total_over(value, sizes, axes):
    groups, ranks, slices = sizes
    if slices != groups:
        return lax.psum(value, axes)
    total = value
    for k in range(1, slices):
        total = total + permute(value, sizes, lambda g, d, t, k=k: (g, d, (t + k) % slices))
    if axes == "tensor":
        return total
    line = total
    for k in range(1, groups * ranks):

        def target(g, d, t, k=k):
            place = (g * ranks + d + k) % (groups * ranks)
            return (place // ranks, place % ranks, t)

        total = total + permute(line, sizes, target)
    return total


def per_device(weight, moment, second, gradient, hidden, stream, norm_gain):
    sizes = tuple(lax.axis_size(axis) for axis in AXES)
    groups, ranks, slices = sizes
    g, d, t = (lax.axis_index(axis) for axis in AXES)
    entries = weight.size * groups * ranks * slices
    width = stream.shape[1] * slices
    rows, units = hidden.shape
    split = slices // groups
    pick = lambda value, place: lax.dynamic_index_in_dim(value, place, 0, keepdims=False)

    moved = permute(
        hidden, sizes, lambda g, d, t: (t // split, d, g * split + t % split)
    )
    if split == 1:
        near = [moved] + [
            permute(moved, sizes, lambda g, d, t, k=k: (g, d, (t + k) % slices))
            for k in range(1, slices)
        ]

    grad_float = gradient.astype(jnp.float32)
    squared = jnp.full((1, 128), jnp.sum(grad_float * grad_float))
    grad_total = total_over(squared, sizes, AXES)[0, 0]
    factor = jnp.minimum(1.0, clip_rms * math.sqrt(entries) / (jnp.sqrt(grad_total) + 1e-06))
    if split == 1:
        factor, *far = lax.optimization_barrier((factor, *near[1:]))
        near = [moved, *far]
    clipped = factor * grad_float
    moment_new = beta_one * moment + (1.0 - beta_one) * clipped
    second_new = beta_two * second + (1.0 - beta_two) * clipped * clipped
    update = moment_new / bias_one / (jnp.sqrt(second_new / bias_two) + adam_eps)
    weight_new = weight - learn_rate * update
    shipped = weight_new.astype(jnp.bfloat16)
    cols = shipped.shape[1]

    if split == 1:
        lots = [jnp.concatenate(near, axis=0)]
        for r in range(1, ranks):
            far = [
                permute(piece, sizes, lambda g, d, t, r=r: (g, (d + r) % ranks, t))
                for piece in near
            ]
            lots.append(jnp.concatenate(far, axis=0))
    else:
        full = lax.all_gather(moved, ("dp", "tensor"), axis=0, tiled=True)
        full = full.reshape(ranks, groups, split, rows, units).transpose(0, 1, 3, 2, 4)
        full = full.reshape(ranks, groups * rows, split * units)
        lots = [pick(full, (d - r) % ranks) for r in range(ranks)]

    sums = []
    for lot in lots:
        term = jnp.dot(lot, shipped, preferred_element_type=jnp.float32)
        part = term.astype(jnp.bfloat16).reshape(groups, rows, cols)
        if split == 1:
            part = jnp.stack([pick(part, (t - place) % groups) for place in range(groups)])
        step = 1
        while step < groups:
            bit = (g // step) % 2
            pairs = part.reshape(-1, 2, rows, cols)
            kept = lax.dynamic_index_in_dim(pairs, bit, 1, keepdims=False)
            sent = lax.dynamic_index_in_dim(pairs, 1 - bit, 1, keepdims=False)
            got = permute(sent, sizes, lambda g, d, t, step=step: (g ^ step, d, t))
            part = (kept.astype(jnp.float32) + got.astype(jnp.float32)).astype(jnp.bfloat16)
            step *= 2
        sums.append(part.reshape(rows, cols))
    sums = jnp.stack(sums)

    place = (d * slices + t) % ranks
    arrived = []
    for turn in range(ranks):

        def target(g, d, t, turn=turn):
            block = d * slices + t
            return (g, (block % ranks + turn) % ranks, block // ranks)

        arrived.append(permute(pick(sums, (d - place - turn) % ranks), sizes, target))
    arrived = jnp.stack(arrived)
    summed = jnp.concatenate([pick(arrived, (d - h) % ranks) for h in range(ranks)], axis=1)

    residual_sum = stream.astype(jnp.float32) + summed.astype(jnp.float32)
    squares = total_over(jnp.sum(residual_sum * residual_sum, axis=1), sizes, "tensor")
    normed = residual_sum * lax.rsqrt(squares / width + 1e-06)[:, None] * norm_gain.astype(jnp.float32)
    return (
        weight_new,
        moment_new,
        second_new,
        normed.astype(jnp.bfloat16),
        residual_sum.astype(jnp.bfloat16),
    )


def solution(mesh):
    master = P("group", ("dp", "tensor"))
    decode = P(("group", "dp"), "tensor")
    return jax.shard_map(
        per_device,
        mesh=mesh,
        in_specs=(master, master, master, master, decode, decode, P("tensor")),
        out_specs=(master, master, master, decode, decode),
        check_vma=False,
    )
```

```python
import math

import jax
import jax.numpy as jnp
from jax import lax
from jax.sharding import PartitionSpec as P

AXES = ("group", "dp", "tensor")

clip_rms = 0.5
beta_one = 0.9
beta_two = 0.95
bias_one = 1.0 - 0.9**10
bias_two = 1.0 - 0.95**10
adam_eps = 1e-08
learn_rate = 0.002


def permute(value, sizes, target):
    groups, ranks, slices = sizes
    index = lambda g, d, t: (g * ranks + d) * slices + t
    pairs = [
        (index(g, d, t), index(*target(g, d, t)))
        for g in range(groups)
        for d in range(ranks)
        for t in range(slices)
    ]
    return lax.ppermute(value, AXES, pairs)


def transpose_hidden(hidden, sizes):
    split = sizes[2] // sizes[0]
    return permute(hidden, sizes, lambda g, d, t: (t // split, d, g * split + t % split))


def gather_hidden(moved, sizes):
    groups, ranks, slices = sizes
    split = slices // groups
    rows, units = moved.shape
    full = lax.all_gather(moved, ("dp", "tensor"), axis=0, tiled=True)
    if split == 1:
        return full
    full = full.reshape(ranks * groups, split, rows, units).transpose(0, 2, 1, 3)
    return full.reshape(ranks * groups * rows, split * units)


def spread(part, sizes):
    groups, ranks, slices = sizes
    g, d, t = (lax.axis_index(axis) for axis in AXES)
    place = (d * slices + t) % ranks
    arrived = []
    for turn in range(ranks):

        def target(g, d, t, turn=turn):
            block = d * slices + t
            return (g, (block % ranks + turn) % ranks, block // ranks)

        sent = lax.dynamic_index_in_dim(part, (place + turn) % ranks, 0, keepdims=False)
        arrived.append(permute(sent, sizes, target))
    arrived = jnp.stack(arrived)
    ordered = [
        lax.dynamic_index_in_dim(arrived, (d - h) % ranks, 0, keepdims=False) for h in range(ranks)
    ]
    return jnp.concatenate(ordered, axis=1)


def per_device(weight, moment, second, gradient, hidden, stream, norm_gain):
    sizes = tuple(lax.axis_size(axis) for axis in AXES)
    groups, ranks, slices = sizes
    g, d, t = (lax.axis_index(axis) for axis in AXES)
    entries = weight.size * groups * ranks * slices
    width = stream.shape[1] * slices
    rows = stream.shape[0]

    lots = 2 if rows % 32 == 0 else 1
    height = rows // lots
    moved = [
        transpose_hidden(hidden[lot * height : (lot + 1) * height], sizes) for lot in range(lots)
    ]

    grad_float = gradient.astype(jnp.float32)
    squared = jnp.sum(grad_float * grad_float)
    squared, moved[-1] = lax.optimization_barrier((squared, moved[-1]))
    activations = [gather_hidden(lot, sizes) for lot in moved]
    grad_total = lax.psum(squared, AXES)
    factor = jnp.minimum(1.0, clip_rms * math.sqrt(entries) / (jnp.sqrt(grad_total) + 1e-06))
    clipped = factor * grad_float
    moment_new = beta_one * moment + (1.0 - beta_one) * clipped
    second_new = beta_two * second + (1.0 - beta_two) * clipped * clipped
    update = moment_new / bias_one / (jnp.sqrt(second_new / bias_two) + adam_eps)
    weight_new = weight - learn_rate * update
    shipped = weight_new.astype(jnp.bfloat16)

    cols = shipped.shape[1]
    summed = []
    part = None
    for lot in activations:
        if part is not None:
            part, lot = lax.optimization_barrier((part, lot))
            summed.append(spread(part, sizes))
        term = jnp.dot(lot, shipped, preferred_element_type=jnp.float32)
        part = term.astype(jnp.bfloat16)

        step = 1
        while step < groups:
            bit = (g // step) % 2
            pairs = part.reshape(-1, 2, height, cols)
            kept = lax.dynamic_index_in_dim(pairs, bit, 1, keepdims=False)
            sent = lax.dynamic_index_in_dim(pairs, 1 - bit, 1, keepdims=False)
            got = permute(sent, sizes, lambda g, d, t, step=step: (g ^ step, d, t))
            part = (kept.astype(jnp.float32) + got.astype(jnp.float32)).astype(jnp.bfloat16)
            step *= 2
        part = part.reshape(ranks, height, cols)
    summed.append(spread(part, sizes))
    summed = jnp.concatenate(summed, axis=0)

    residual_sum = stream.astype(jnp.float32) + summed.astype(jnp.float32)
    squares = lax.psum(jnp.sum(residual_sum * residual_sum, axis=1), "tensor")
    normed = residual_sum * lax.rsqrt(squares / width + 1e-06)[:, None] * norm_gain.astype(jnp.float32)
    return (
        weight_new,
        moment_new,
        second_new,
        normed.astype(jnp.bfloat16),
        residual_sum.astype(jnp.bfloat16),
    )


def solution(mesh):
    master = P("group", ("dp", "tensor"))
    decode = P(("group", "dp"), "tensor")
    return jax.shard_map(
        per_device,
        mesh=mesh,
        in_specs=(master, master, master, master, decode, decode, P("tensor")),
        out_specs=(master, master, master, decode, decode),
        check_vma=False,
    )
```
